256 devices in a mesh: ctx: 16 (over x_hi, z), head: 16 (over y, x_lo, core).
Axes of the slice: x: 4 (x_hi: 2, x_lo: 2; x = x_hi * 2 + x_lo), y: 4, z: 8, core: 2. Of those that a mesh axis runs over, the one named last changes fastest.
Arguments:
- queries: bfloat16 [6144, 32, 128], P('ctx', 'head'), may hold values from -72 to 72
- codes: int32 [6144, 128], P('ctx'), may hold values from 0 to 255
- codebook_k: bfloat16 [8, 256, 128], replicated, may hold values from -6 to 6
- codebook_v: bfloat16 [8, 256, 128], replicated, may hold values from -6 to 6
- grad_out: bfloat16 [6144, 32, 128], P('ctx', 'head'), may hold values from -12 to 12
Outputs:
- attention: bfloat16 [6144, 32, 128], P('ctx', 'head')
- query_grad: bfloat16 [6144, 32, 128], P('ctx', 'head')
- book_grad_k: float32 [8, 256, 128], P(None, 'ctx', 'head')
- book_grad_v: float32 [8, 256, 128], P(None, 'ctx', 'head')
The draws below stay inside these ranges and needn't reach their ends.
All inputs are finite; a program needn't handle non-finite values.
Results may differ from the reference program's by a relative error of at most 0.04.
Values may be sent and summed in bfloat16 or wider, within the bound.
No kernel may reach another device: no remote copies, remote signals or barrier semaphores. Data moves between devices by JAX's collectives and lax.ppermute only.
A program may use at most 64 MiB of HBM per device.

```python
import math
import jax
import jax.numpy as jnp
from jax import lax

HQ = 32
KVH = 8
HD = 128
SUB = 16
CODES = 256
GROUP = 4
SEQ = 6144


def draw_queries(key, part):
    key = jax.random.fold_in(key, 17)
    normal_key = jax.random.fold_in(key, 0)
    normal_part = jax.random.truncated_normal(normal_key, -6.0, 6.0, (SEQ, HQ, HD), jnp.float32)
    return normal_part.astype(jnp.bfloat16)


def draw_grad_out(key, part):
    key = jax.random.fold_in(key, 29)
    normal_part = jax.random.truncated_normal(key, -6.0, 6.0, (SEQ, HQ, HD), jnp.float32)
    positions = jnp.arange(SEQ, dtype=jnp.float32) / (SEQ - 1)
    row_scale = 0.5 + 1.5 * positions
    return (normal_part * row_scale[:, None, None]).astype(jnp.bfloat16)


def place_ends(values, rng, least, high):
    extent = values.shape
    place = [jax.random.randint(jax.random.fold_in(rng, axis), (), 0, extent[axis]) for axis in range(len(extent))]
    values = values.at[tuple(place)].set(least)
    longest = extent.index(max(extent))
    place[longest] = (place[longest] + 1) % extent[longest]
    return values.at[tuple(place)].set(high)


def noise(key, extent, spread, most, kind=jnp.bfloat16):
    array = jax.random.normal(key, extent, jnp.float32) * spread
    return jnp.minimum(jnp.maximum(array, -most), most).astype(kind)


def setup_inputs(seed: int = 0) -> dict:
    key_list = jax.random.split(jax.random.key(seed), 6)
    queries = draw_queries(jax.random.fold_in(key_list[5], 71), 0)
    codes = place_ends(jax.random.randint(key_list[1], (SEQ, KVH * SUB), 0, CODES), jax.random.fold_in(key_list[1], 1), 0, CODES - 1).astype(jnp.int32)
    codebook_k = noise(key_list[2], (KVH, CODES, HD), 1.0, 6.0)
    codebook_v = noise(key_list[3], (KVH, CODES, HD), 1.0, 6.0)
    grad_out = draw_grad_out(jax.random.fold_in(key_list[5], 71), 0)
    return {"queries": queries, "codes": codes, "codebook_k": codebook_k, "codebook_v": codebook_v, "grad_out": grad_out}


NEGATIVE = -1.0e30


def decode_head(code_rows, book):
    levels = jnp.arange(CODES, dtype=jnp.int32)
    onehot = (code_rows[:, :, None] == levels[None, None, :]).astype(jnp.float32)
    tables = book.astype(jnp.float32).reshape(CODES, SUB, HD // SUB)
    decoded = jnp.einsum("tsc,csj->tsj", onehot, tables, precision=lax.Precision.HIGHEST)
    return decoded.reshape(SEQ, HD).astype(jnp.bfloat16)


def book_gradient(code_rows, gradient):
    levels = jnp.arange(CODES, dtype=jnp.int32)
    onehot = (code_rows[:, :, None] == levels[None, None, :]).astype(jnp.float32)
    tables = gradient.reshape(SEQ, SUB, HD // SUB)
    summed = jnp.einsum("tsc,tsj->csj", onehot, tables, precision=lax.Precision.HIGHEST)
    return summed.reshape(CODES, HD)


def reference(queries, codes, codebook_k, codebook_v, grad_out):
    score_scale = HD ** -0.5
    block_size = math.gcd(SEQ, 512)
    block_count = SEQ // block_size
    query_heads = jnp.transpose(queries, (1, 0, 2)).reshape(KVH, GROUP, SEQ, HD)
    grad_heads = jnp.transpose(grad_out, (1, 0, 2)).reshape(KVH, GROUP, SEQ, HD)
    code_heads = jnp.transpose(codes.reshape(SEQ, KVH, SUB), (1, 0, 2))
    key_positions = jnp.arange(SEQ, dtype=jnp.int32)

    def per_kv(element):
        code_rows, book_k, book_v, query_group, grad_group = element
        key_rows = decode_head(code_rows, book_k)
        values = decode_head(code_rows, book_v)

        def one_block(running, element_two):
            block_index, query_block, grad_block = element_two
            grad_keys, grad_values = running
            query_positions = block_index * block_size + jnp.arange(block_size, dtype=jnp.int32)
            allowed = key_positions[None, :] <= query_positions[:, None]
            scores = jnp.dot(query_block, key_rows.T, preferred_element_type=jnp.float32) * score_scale
            scores = jnp.where(allowed, scores, NEGATIVE)
            highest = jnp.max(scores, axis=1)
            denominator = jnp.sum(jnp.where(allowed, jnp.exp(scores - highest[:, None]), 0.0), axis=1)
            log_total = highest + jnp.log(denominator)
            attention_weight_matrix = jnp.where(allowed, jnp.exp(scores - log_total[:, None]), 0.0)
            rounded = attention_weight_matrix.astype(jnp.bfloat16)
            output = jnp.dot(rounded, values, preferred_element_type=jnp.float32).astype(jnp.bfloat16)
            correction = jnp.sum(grad_block.astype(jnp.float32) * output.astype(jnp.float32), axis=1)
            products = jnp.dot(grad_block, values.T, preferred_element_type=jnp.float32)
            linear_bias_slopes = (attention_weight_matrix * (products - correction[:, None])).astype(jnp.bfloat16)
            grad_query = (jnp.dot(linear_bias_slopes, key_rows, preferred_element_type=jnp.float32) * score_scale).astype(jnp.bfloat16)
            grad_keys = grad_keys + jnp.dot(linear_bias_slopes.T, query_block, preferred_element_type=jnp.float32) * score_scale
            grad_values = grad_values + jnp.dot(rounded.T, grad_block, preferred_element_type=jnp.float32)
            return (grad_keys, grad_values), (output, grad_query)

        def per_query_head(running, pair_rows):
            query_rows, grad_rows = pair_rows
            running, (outputs, grad_queries) = lax.scan(
                one_block, running,
                (jnp.arange(block_count, dtype=jnp.int32),
                 query_rows.reshape(block_count, block_size, HD),
                 grad_rows.reshape(block_count, block_size, HD)))
            return running, (outputs.reshape(SEQ, HD), grad_queries.reshape(SEQ, HD))

        zeros_rows = jnp.zeros((SEQ, HD), jnp.float32)
        (grad_keys, grad_values), (outputs, grad_queries) = lax.scan(
            per_query_head, (zeros_rows, zeros_rows), (query_group, grad_group))
        return outputs, grad_queries, book_gradient(code_rows, grad_keys), book_gradient(code_rows, grad_values)

    outputs, grad_queries, books_k, books_v = lax.map(
        per_kv, (code_heads, codebook_k, codebook_v, query_heads, grad_heads))
    attention = jnp.transpose(outputs.reshape(HQ, SEQ, HD), (1, 0, 2))
    query_grad = jnp.transpose(grad_queries.reshape(HQ, SEQ, HD), (1, 0, 2))
    return attention, query_grad, books_k, books_v
```

```python
import functools
import jax
import jax.numpy as jnp
from jax import lax
from jax.experimental import pallas as pl
from jax.experimental.pallas import tpu as pltpu
from jax.sharding import PartitionSpec as P

KVH = 8
HD = 128
SUB = 16
CODES = 256
GROUP = 4
COLS = HD // SUB
HEADS = 2
TILE = 256
LANES = 128
NEGATIVE = -1e30
SCALE = HD ** -0.5
LOG2E = 1.4426950408889634
F32 = jnp.float32
BF = jnp.bfloat16


def nn(a, b):
    return lax.dot_general(a, b, (((1,), (0,)), ((), ())), preferred_element_type=F32)


def nt(a, b):
    return lax.dot_general(a, b, (((1,), (1,)), ((), ())), preferred_element_type=F32)


def kernel(meta, q_ref, g_ref, codes_ref, bk_ref, bv_ref, attn_ref, qg_ref, book_ref,
           s_ref, kt_ref, vt_ref, tk_ref, tv_ref, m_ref, l_ref, c_ref, o_ref, dq_ref, acc_ref,
           qt_ref, gt_ref, x_ref):
    rows = q_ref.shape[0]
    own_first = meta[0]
    kv = meta[1]
    n_full = own_first // TILE
    n_all = (own_first + rows // HEADS + TILE - 1) // TILE
    tk_ref[...] = bk_ref[kv].astype(F32).T
    tv_ref[...] = bv_ref[kv].astype(F32).T
    qt_ref[...] = q_ref[...].astype(F32).T.astype(BF)
    gt_ref[...] = g_ref[...].astype(F32).T.astype(BF)
    m_ref[...] = jnp.full((rows, LANES), NEGATIVE, F32)
    l_ref[...] = jnp.zeros((rows, LANES), F32)
    o_ref[...] = jnp.zeros((rows, HD), F32)
    dq_ref[...] = jnp.zeros((rows, HD), F32)
    acc_ref[...] = jnp.zeros(acc_ref.shape, F32)
    x_ref[...] = jnp.zeros(x_ref.shape, BF)

    def decode(j):
        for half in range(2):
            codes = codes_ref[2 * j + half]
            for s in range(SUB):
                idx = jnp.broadcast_to(codes[s:s + 1], (COLS, LANES))
                low = idx & (LANES - 1)
                upper = idx >= LANES
                r = slice(s * COLS, (s + 1) * COLS)
                for t_ref, out in ((tk_ref, kt_ref), (tv_ref, vt_ref)):
                    a = jnp.take_along_axis(t_ref[r, :LANES], low, axis=1, mode="promise_in_bounds")
                    b = jnp.take_along_axis(t_ref[r, LANES:], low, axis=1, mode="promise_in_bounds")
                    out[j, r, half * LANES:(half + 1) * LANES] = jnp.where(upper, b, a).astype(BF)

    chunks = [slice(c, c + 256) for c in range(0, rows, 256)]

    def scores(j, masked):
        kt = kt_ref[j]
        for c in chunks:
            s = nn(q_ref[c], kt) * (SCALE * LOG2E)
            if masked:
                u = j * TILE + lax.broadcasted_iota(jnp.int32, s.shape, 1)
                t = own_first + (c.start + lax.broadcasted_iota(jnp.int32, s.shape, 0)) // HEADS
                s = jnp.where(u <= t, s, NEGATIVE)
            s_ref[j, c] = s
            m_ref[c] = jnp.maximum(m_ref[c], jnp.maximum(s[:, :LANES], s[:, LANES:]))

    def step_a(j, masked):
        decode(j)
        scores(j, masked)

    lax.fori_loop(0, n_full, lambda j, _: (step_a(j, False), 0)[1], 0)
    lax.fori_loop(n_full, n_all, lambda j, _: (step_a(j, True), 0)[1], 0)
    for c in chunks:
        m_ref[c] = jnp.broadcast_to(jnp.max(m_ref[c], axis=1, keepdims=True), (256, LANES))

    def step_b(j, _):
        vt = vt_ref[j]
        for c in chunks:
            m = m_ref[c]
            s = s_ref[j, c]
            e0 = jnp.exp2(s[:, :LANES] - m)
            e1 = jnp.exp2(s[:, LANES:] - m)
            l_ref[c] = l_ref[c] + (e0 + e1)
            e = jnp.concatenate([e0, e1], axis=1).astype(BF)
            o_ref[c] += nt(e, vt)
        return 0

    lax.fori_loop(0, n_all, step_b, 0)
    for c in chunks:
        total = jnp.sum(l_ref[c], axis=1, keepdims=True)
        out = (o_ref[c] / total).astype(BF)
        attn_ref[c] = out
        fix = jnp.sum(g_ref[c].astype(F32) * out.astype(F32), axis=1, keepdims=True)
        c_ref[c] = jnp.broadcast_to(fix, (256, LANES))
        m_ref[c] = m_ref[c] + jnp.log2(total)

    hi_iota = lax.broadcasted_iota(jnp.int32, (64, TILE), 0).astype(F32).astype(BF)
    one, zero = jnp.ones((64, TILE), BF), jnp.zeros((64, TILE), BF)
    zx = jnp.zeros((2 * COLS, TILE), BF)

    def code_sums(j):
        codes = jnp.concatenate([codes_ref[2 * j], codes_ref[2 * j + 1]], axis=1)
        high = (((codes >> 2) & 3) * 16 + (codes >> 4)).astype(F32).astype(BF)
        low = (codes & 3).astype(F32).astype(BF)
        for grp in range(4):
            his, xs = [], []
            for s in range(4 * grp, 4 * grp + 4):
                his.append(jnp.where(hi_iota == jnp.broadcast_to(high[s:s + 1], (64, TILE)), one, zero))
                x = x_ref[s * 16:(s + 1) * 16]
                lo = jnp.broadcast_to(low[s:s + 1], (16, TILE))
                for v in range(4):
                    xs.append(jnp.where(lo == jnp.full((16, TILE), v, BF), x, zx))
            acc_ref[grp] += nt(jnp.concatenate(his, axis=0), jnp.concatenate(xs, axis=0))

    def step_c(j, _):
        code_sums(jnp.maximum(j - 1, 0))
        vt, kt = vt_ref[j], kt_ref[j]
        dv = jnp.zeros((HD, TILE), F32)
        dk = jnp.zeros((HD, TILE), F32)
        for c in chunks:
            lse, fix = m_ref[c], c_ref[c]
            s = s_ref[j, c]
            w = jnp.exp2(s - jnp.concatenate([lse, lse], axis=1))
            dp = nn(g_ref[c], vt)
            ds = (w * (dp - jnp.concatenate([fix, fix], axis=1))).astype(BF)
            dq_ref[c] += nt(ds, kt)
            dv += nn(gt_ref[:, c], w.astype(BF))
            dk += nn(qt_ref[:, c], ds)
        dk = dk * SCALE
        for s in range(SUB):
            r = slice(s * COLS, (s + 1) * COLS)
            x_ref[s * 16:(s + 1) * 16] = jnp.concatenate([dk[r], dv[r]], axis=0).astype(BF)
        return 0

    lax.fori_loop(0, n_all, step_c, 0)
    code_sums(n_all - 1)
    qg_ref[...] = (dq_ref[...] * SCALE).astype(BF)
    for s in range(SUB):
        a = acc_ref[s // 4, (s % 4) * 64:(s % 4 + 1) * 64, (s % 4) * 64:(s % 4 + 1) * 64].astype(BF)
        for q in range(4):
            book_ref[s * 16:(s + 1) * 16, q * 64:(q + 1) * 64] = a[q * 16:(q + 1) * 16]


def attend(meta, q, g, codes, bk, bv):
    rows = q.shape[0]
    tiles = codes.shape[0] // 2
    vm = pl.BlockSpec(memory_space=pltpu.VMEM)
    return pl.pallas_call(
        kernel,
        out_shape=(jax.ShapeDtypeStruct((rows, HD), BF), jax.ShapeDtypeStruct((rows, HD), BF),
                   jax.ShapeDtypeStruct((CODES, 2 * HD), BF)),
        in_specs=[pl.BlockSpec(memory_space=pltpu.SMEM)] + [vm] * 5,
        out_specs=[vm] * 3,
        scratch_shapes=[
            pltpu.VMEM((tiles, rows, TILE), F32),
            pltpu.VMEM((tiles, HD, TILE), BF),
            pltpu.VMEM((tiles, HD, TILE), BF),
            pltpu.VMEM((HD, CODES), F32),
            pltpu.VMEM((HD, CODES), F32),
            pltpu.VMEM((rows, LANES), F32),
            pltpu.VMEM((rows, LANES), F32),
            pltpu.VMEM((rows, LANES), F32),
            pltpu.VMEM((rows, HD), F32),
            pltpu.VMEM((rows, HD), F32),
            pltpu.VMEM((4, 256, 256), F32),
            pltpu.VMEM((HD, rows), BF),
            pltpu.VMEM((HD, rows), BF),
            pltpu.VMEM((CODES, TILE), BF),
        ],
        compiler_params=pltpu.CompilerParams(vmem_limit_bytes=48 * 1024 * 1024),
    )(meta, q, g, codes, bk, bv)


def per_device(queries, codes, codebook_k, codebook_v, grad_out):
    row_count, head_count, columns = queries.shape
    n_ctx, n_head = lax.axis_size("ctx"), lax.axis_size("head")
    kv = lax.axis_index("head") * head_count // GROUP
    own_first = lax.axis_index("ctx") * row_count
    own_codes = lax.dynamic_slice_in_dim(codes, kv * SUB, SUB, 1)
    own_codes = own_codes.reshape(row_count // LANES, LANES, SUB).transpose(0, 2, 1)
    spread = jnp.broadcast_to(own_codes[None], (n_ctx,) + own_codes.shape)
    all_codes = lax.all_to_all(spread, "ctx", 0, 0).reshape(-1, SUB, LANES)
    meta = jnp.stack([own_first, kv]).astype(jnp.int32)
    attention, query_grad, books = attend(
        meta,
        queries.reshape(-1, columns),
        grad_out.reshape(-1, columns),
        all_codes,
        codebook_k,
        codebook_v,
    )
    parts = lax.all_to_all(books, ("head", "ctx"), 0, 0, tiled=True)
    sums = jnp.sum(parts.astype(F32).reshape(KVH, -1, parts.shape[1]), axis=1)
    sums = sums.reshape(KVH, CODES // n_ctx, 2, columns // n_head)
    return (
        attention.reshape(queries.shape),
        query_grad.reshape(queries.shape),
        sums[:, :, 0],
        sums[:, :, 1],
    )


def solution(mesh):
    placed = (P("ctx", "head", None), P("ctx", None), P(), P(), P("ctx", "head", None))
    return jax.shard_map(
        per_device,
        mesh=mesh,
        in_specs=placed,
        out_specs=(
            P("ctx", "head", None),
            P("ctx", "head", None),
            P(None, "ctx", "head"),
            P(None, "ctx", "head"),
        ),
        check_vma=False,
    )
```

```python
import functools
import jax
import jax.numpy as jnp
from jax import lax
from jax.experimental import pallas as pl
from jax.experimental.pallas import tpu as pltpu
from jax.sharding import PartitionSpec as P

KVH = 8
HD = 128
SUB = 16
CODES = 256
GROUP = 4
COLS = HD // SUB
HEADS = 2
TILE = 512
PARTS = 3
WIDE = PARTS * TILE
CHUNK = 384
LANES = 128
NEGATIVE = -1e30
SCALE = HD ** -0.5
LOG2E = 1.4426950408889634
F32 = jnp.float32
BF = jnp.bfloat16


def nn(a, b):
    return lax.dot_general(a, b, (((1,), (0,)), ((), ())), preferred_element_type=F32)


def nt(a, b):
    return lax.dot_general(a, b, (((1,), (1,)), ((), ())), preferred_element_type=F32)


def kernel(meta, q_ref, g_ref, codes_ref, bk_ref, bv_ref, attn_ref, qg_ref, book_ref,
           s_ref, kt_ref, vt_ref, next_ref, tk_ref, tv_ref, m_ref, l_ref, c_ref, o_ref, dq_ref, acc_ref,
           qt_ref, gt_ref, *bufs):
    rows = q_ref.shape[0]
    own_first = meta[0]
    kv = meta[1]
    n_all = (own_first + rows // HEADS + WIDE - 1) // WIDE
    last = n_all - 1
    w_refs, d_refs, x_refs = bufs[:PARTS], bufs[PARTS:2 * PARTS], bufs[2 * PARTS:]
    tk_ref[...] = bk_ref[kv].astype(F32).T
    tv_ref[...] = bv_ref[kv].astype(F32).T
    qt_ref[...] = q_ref[...].astype(F32).T.astype(BF)
    gt_ref[...] = g_ref[...].astype(F32).T.astype(BF)
    m_ref[...] = jnp.full((rows, LANES), NEGATIVE, F32)
    l_ref[...] = jnp.zeros((rows, LANES), F32)
    o_ref[...] = jnp.zeros((rows, HD), F32)
    dq_ref[...] = jnp.zeros((rows, HD), F32)
    acc_ref[...] = jnp.zeros(acc_ref.shape, F32)
    for ref in (w_refs[-1], d_refs[-1], *x_refs[-2:]):
        ref[...] = jnp.zeros(ref.shape, BF)

    def decode(j, t_ref, out):
        for part in range(WIDE // LANES):
            codes = codes_ref[j * (WIDE // LANES) + part]
            for s in range(SUB):
                idx = jnp.broadcast_to(codes[s:s + 1], (COLS, LANES))
                low = idx & (LANES - 1)
                upper = idx >= LANES
                r = slice(s * COLS, (s + 1) * COLS)
                a = jnp.take_along_axis(t_ref[r, :LANES], low, axis=1, mode="promise_in_bounds")
                b = jnp.take_along_axis(t_ref[r, LANES:], low, axis=1, mode="promise_in_bounds")
                out[r, part * LANES:(part + 1) * LANES] = jnp.where(upper, b, a).astype(BF)

    chunks = [slice(c, c + CHUNK) for c in range(0, rows, CHUNK)]
    parts = [slice(p * TILE, (p + 1) * TILE) for p in range(PARTS)]

    def scores(j, masked):
        for c in chunks:
            top = m_ref[c]
            for p in parts:
                s = nn(q_ref[c], kt_ref[j, :, p]) * (SCALE * LOG2E)
                if masked:
                    u = j * WIDE + p.start + lax.broadcasted_iota(jnp.int32, s.shape, 1)
                    t = own_first + (c.start + lax.broadcasted_iota(jnp.int32, s.shape, 0)) // HEADS
                    s = jnp.where(u <= t, s, NEGATIVE)
                s_ref[j, c, p] = s
                for lane in range(0, TILE, LANES):
                    top = jnp.maximum(top, s[:, lane:lane + LANES])
            m_ref[c] = top

    def step_a(j, _):
        scores(j, False)
        decode(j + 1, tk_ref, next_ref)
        kt_ref[j + 1] = next_ref[...]
        return 0

    decode(0, tk_ref, next_ref)
    kt_ref[0] = next_ref[...]
    lax.fori_loop(0, last, step_a, 0)
    scores(last, True)
    decode(0, tv_ref, next_ref)
    vt_ref[0] = next_ref[...]
    for c in chunks:
        m_ref[c] = jnp.broadcast_to(jnp.max(m_ref[c], axis=1, keepdims=True), (CHUNK, LANES))

    def step_b(j, more):
        for c in chunks:
            m = m_ref[c]
            total = l_ref[c]
            es = []
            for p in range(0, WIDE, LANES):
                e = jnp.exp2(s_ref[j, c, p:p + LANES] - m)
                total = total + e
                es.append(e)
            l_ref[c] = total
            o_ref[c] += nt(jnp.concatenate(es, axis=1).astype(BF), vt_ref[j])
        if more:
            decode(j + 1, tv_ref, next_ref)
            vt_ref[j + 1] = next_ref[...]
        return 0

    lax.fori_loop(0, last, lambda j, _: step_b(j, True), 0)
    step_b(last, False)
    for c in chunks:
        total = jnp.sum(l_ref[c], axis=1, keepdims=True)
        out = (o_ref[c] / total).astype(BF)
        attn_ref[c] = out
        fix = jnp.sum(g_ref[c].astype(F32) * out.astype(F32), axis=1, keepdims=True)
        c_ref[c] = jnp.broadcast_to(fix, (CHUNK, LANES))
        m_ref[c] = m_ref[c] + jnp.log2(total)

    hi_iota = lax.broadcasted_iota(jnp.int32, (64, TILE), 0).astype(F32).astype(BF)
    one, zero = jnp.ones((64, TILE), BF), jnp.zeros((64, TILE), BF)
    zx = jnp.zeros((2 * COLS, TILE), BF)

    def code_sums(j, p):
        base = (j * WIDE + p * TILE) // LANES
        codes = jnp.concatenate([codes_ref[base + i] for i in range(TILE // LANES)], axis=1)
        high = (((codes >> 2) & 1) * 32 + (codes >> 4) * 2 + ((codes >> 3) & 1)).astype(F32).astype(BF)
        low = (codes & 3).astype(F32).astype(BF)
        for grp in range(4):
            his, xs = [], []
            for s in range(4 * grp, 4 * grp + 4):
                his.append(jnp.where(hi_iota == jnp.broadcast_to(high[s:s + 1], (64, TILE)), one, zero))
                x = x_refs[p][s * 16:(s + 1) * 16]
                lo = jnp.broadcast_to(low[s:s + 1], (16, TILE))
                for v in range(4):
                    xs.append(jnp.where(lo == jnp.full((16, TILE), v, BF), x, zx))
            acc_ref[grp] += nt(jnp.concatenate(his, axis=0), jnp.concatenate(xs, axis=0))

    def slopes(j, p):
        for c in chunks:
            lse, fix = m_ref[c], c_ref[c]
            w = jnp.exp2(s_ref[j, c, parts[p]] - jnp.concatenate([lse] * (TILE // LANES), axis=1))
            dp = nn(g_ref[c], vt_ref[j, :, parts[p]])
            w_refs[p][c] = w.astype(BF)
            d_refs[p][c] = (w * (dp - jnp.concatenate([fix] * (TILE // LANES), axis=1))).astype(BF)

    def products(j, p):
        for c in chunks:
            dq_ref[c] += nt(d_refs[p][c], kt_ref[j, :, parts[p]])
        dv = nn(gt_ref[...], w_refs[p][...])
        dk = nn(qt_ref[...], d_refs[p][...]) * SCALE
        for s in range(SUB):
            r = slice(s * COLS, (s + 1) * COLS)
            x_refs[p][s * 16:(s + 1) * 16] = jnp.concatenate([dk[r], dv[r]], axis=0).astype(BF)

    def step_c(j, _):
        before = jnp.maximum(j - 1, 0)
        for p in range(PARTS):
            code_sums(before if p < 2 else j, (p - 2) % PARTS)
            products(before if p < 1 else j, (p - 1) % PARTS)
            slopes(j, p)
        return 0

    lax.fori_loop(0, n_all, step_c, 0)
    products(last, PARTS - 1)
    code_sums(last, PARTS - 2)
    code_sums(last, PARTS - 1)
    qg_ref[...] = (dq_ref[...] * SCALE).astype(BF)
    for s in range(SUB):
        at = s % 4 * 64
        a = acc_ref[s // 4, at:at + 64, at:at + 64].astype(BF)
        book_ref[s * 32:(s + 1) * 32] = jnp.concatenate([a[:32], a[32:]], axis=1)


def attend(meta, q, g, codes, bk, bv):
    rows = q.shape[0]
    tiles = codes.shape[0] * LANES // WIDE
    vm = pl.BlockSpec(memory_space=pltpu.VMEM)
    return pl.pallas_call(
        kernel,
        out_shape=(jax.ShapeDtypeStruct((rows, HD), BF), jax.ShapeDtypeStruct((rows, HD), BF),
                   jax.ShapeDtypeStruct((2 * CODES, HD), BF)),
        in_specs=[pl.BlockSpec(memory_space=pltpu.SMEM)] + [vm] * 5,
        out_specs=[vm] * 3,
        scratch_shapes=[
            pltpu.VMEM((tiles, rows, WIDE), F32),
            pltpu.VMEM((tiles, HD, WIDE), BF),
            pltpu.VMEM((tiles, HD, WIDE), BF),
            pltpu.VMEM((HD, WIDE), BF),
            pltpu.VMEM((HD, CODES), F32),
            pltpu.VMEM((HD, CODES), F32),
            pltpu.VMEM((rows, LANES), F32),
            pltpu.VMEM((rows, LANES), F32),
            pltpu.VMEM((rows, LANES), F32),
            pltpu.VMEM((rows, HD), F32),
            pltpu.VMEM((rows, HD), F32),
            pltpu.VMEM((4, 256, 256), F32),
            pltpu.VMEM((HD, rows), BF),
            pltpu.VMEM((HD, rows), BF),
        ]
        + [pltpu.VMEM((rows, TILE), BF)] * (2 * PARTS)
        + [pltpu.VMEM((CODES, TILE), BF)] * PARTS,
        compiler_params=pltpu.CompilerParams(vmem_limit_bytes=48 * 1024 * 1024),
    )(meta, q, g, codes, bk, bv)


def gather_sums(parts_ref, k_ref, v_ref):
    n = parts_ref.shape[0]
    pair = n // KVH
    row = lax.broadcasted_iota(jnp.int32, (KVH, n), 1)
    head = lax.broadcasted_iota(jnp.int32, (KVH, n), 0)
    src = lax.broadcasted_iota(jnp.int32, (HD, HD), 0)
    dst = lax.broadcasted_iota(jnp.int32, (HD, HD), 1)
    parts = parts_ref[...]
    halves = []
    for k in range(2):
        pick = ((row // pair == head) & (row % 2 == k)).astype(F32).astype(BF)
        halves.append(nn(pick, parts))
    for side, out in enumerate((k_ref, v_ref)):
        total = jnp.zeros((KVH, HD), F32)
        for k in range(2):
            want = src % 8 * 16 + 8 * k + src // 16
            place = ((dst == want) & (src // 8 % 2 == side)).astype(F32)
            total += lax.dot_general(halves[k], place, (((1,), (0,)), ((), ())), precision=lax.Precision.HIGHEST, preferred_element_type=F32)
        for j in range(COLS):
            out[:, j, :] = total[:, j * 16:(j + 1) * 16]


def finish(parts):
    vm = pl.BlockSpec(memory_space=pltpu.VMEM)
    shape = jax.ShapeDtypeStruct((KVH, COLS, 16), F32)
    return pl.pallas_call(gather_sums, out_shape=(shape, shape), in_specs=[vm], out_specs=(vm, vm))(parts)


def per_device(queries, codes, codebook_k, codebook_v, grad_out):
    row_count, head_count, columns = queries.shape
    n_ctx, n_head = lax.axis_size("ctx"), lax.axis_size("head")
    kv = lax.axis_index("head") * head_count // GROUP
    own_first = lax.axis_index("ctx") * row_count
    own_codes = lax.dynamic_slice_in_dim(codes, kv * SUB, SUB, 1)
    own_codes = own_codes.reshape(row_count // LANES, LANES, SUB).transpose(0, 2, 1)
    own_codes = own_codes.reshape(-1, LANES).astype(BF)
    spread = jnp.broadcast_to(own_codes[None], (n_ctx,) + own_codes.shape)
    all_codes = lax.all_to_all(spread, "ctx", 0, 0, tiled=True).astype(jnp.int32).reshape(-1, SUB, LANES)
    meta = jnp.stack([own_first, kv]).astype(jnp.int32)
    attention, query_grad, books = attend(
        meta,
        queries.reshape(-1, columns),
        grad_out.reshape(-1, columns),
        all_codes,
        codebook_k,
        codebook_v,
    )
    parts = lax.all_to_all(books.reshape(CODES, 2, columns), ("head", "ctx"), 0, 0, tiled=True)
    sums_k, sums_v = finish(parts.reshape(books.shape))
    return (
        attention.reshape(queries.shape),
        query_grad.reshape(queries.shape),
        sums_k.transpose(0, 2, 1),
        sums_v.transpose(0, 2, 1),
    )


def solution(mesh):
    placed = (P("ctx", "head", None), P("ctx", None), P(), P(), P("ctx", "head", None))
    return jax.shard_map(
        per_device,
        mesh=mesh,
        in_specs=placed,
        out_specs=(
            P("ctx", "head", None),
            P("ctx", "head", None),
            P(None, "ctx", "head"),
            P(None, "ctx", "head"),
        ),
        check_vma=False,
    )
```

```python
import functools
import jax
import jax.numpy as jnp
from jax import lax
from jax.experimental import pallas as pl
from jax.experimental.pallas import tpu as pltpu
from jax.sharding import PartitionSpec as P

KVH = 8
HD = 128
SUB = 16
CODES = 256
GROUP = 4
COLS = HD // SUB
HEADS = 2
TILE = 512
PARTS = 3
WIDE = PARTS * TILE
CHUNK = 384
LANES = 128
NEGATIVE = -1e30
SCALE = HD ** -0.5
LOG2E = 1.4426950408889634
F32 = jnp.float32
BF = jnp.bfloat16


def nn(a, b):
    return lax.dot_general(a, b, (((1,), (0,)), ((), ())), preferred_element_type=F32)


def nt(a, b):
    return lax.dot_general(a, b, (((1,), (1,)), ((), ())), preferred_element_type=F32)


def kernel(q_ref, g_ref, codes_ref, bk_ref, bv_ref, attn_ref, qg_ref, book_ref,
           s_ref, kt_ref, vt_ref, next_ref, tk_ref, tv_ref, m_ref, l_ref, c_ref, o_ref, dq_ref, acc_ref,
           qt_ref, gt_ref, *bufs):
    rows = q_ref.shape[0]
    own_first = lax.axis_index("ctx") * (rows // HEADS)
    kv = lax.axis_index("head") * HEADS // GROUP
    n_all = (own_first + rows // HEADS + WIDE - 1) // WIDE
    last = n_all - 1
    w_refs, d_refs, x_refs = bufs[:PARTS], bufs[PARTS:2 * PARTS], bufs[2 * PARTS:]
    tk_ref[...] = bk_ref[kv].astype(F32).T
    tv_ref[...] = bv_ref[kv].astype(F32).T
    qt_ref[...] = q_ref[...].astype(F32).T.astype(BF)
    gt_ref[...] = g_ref[...].astype(F32).T.astype(BF)
    m_ref[...] = jnp.full((rows, LANES), NEGATIVE, F32)
    l_ref[...] = jnp.zeros((rows, LANES), F32)
    o_ref[...] = jnp.zeros((rows, HD), F32)

    def decode(j, t_ref, out):
        for part in range(WIDE // LANES):
            codes = codes_ref[j * (WIDE // LANES) + part]
            for s in range(SUB):
                idx = jnp.broadcast_to(codes[s:s + 1], (COLS, LANES))
                low = idx & (LANES - 1)
                upper = idx >= LANES
                r = slice(s * COLS, (s + 1) * COLS)
                a = jnp.take_along_axis(t_ref[r, :LANES], low, axis=1, mode="promise_in_bounds")
                b = jnp.take_along_axis(t_ref[r, LANES:], low, axis=1, mode="promise_in_bounds")
                out[r, part * LANES:(part + 1) * LANES] = jnp.where(upper, b, a).astype(BF)

    chunks = [slice(c, c + CHUNK) for c in range(0, rows, CHUNK)]
    parts = [slice(p * TILE, (p + 1) * TILE) for p in range(PARTS)]

    def scores(j, masked):
        for c in chunks:
            top = m_ref[c]
            for p in parts:
                s = nn(q_ref[c], kt_ref[j, :, p]) * (SCALE * LOG2E)
                if masked:
                    u = j * WIDE + p.start + lax.broadcasted_iota(jnp.int32, s.shape, 1)
                    t = own_first + (c.start + lax.broadcasted_iota(jnp.int32, s.shape, 0)) // HEADS
                    s = jnp.where(u <= t, s, NEGATIVE)
                s_ref[j, c, p] = s
                for lane in range(0, TILE, LANES):
                    top = jnp.maximum(top, s[:, lane:lane + LANES])
            m_ref[c] = top

    def step_a(j, _):
        scores(j, False)
        decode(j + 1, tk_ref, next_ref)
        kt_ref[j + 1] = next_ref[...]
        return 0

    decode(0, tk_ref, next_ref)
    kt_ref[0] = next_ref[...]
    lax.fori_loop(0, last, step_a, 0)
    scores(last, True)
    decode(0, tv_ref, next_ref)
    vt_ref[0] = next_ref[...]
    for c in chunks:
        m_ref[c] = jnp.broadcast_to(jnp.max(m_ref[c], axis=1, keepdims=True), (CHUNK, LANES))

    def step_b(j, more):
        for c in chunks:
            m = m_ref[c]
            total = l_ref[c]
            es = []
            for p in range(0, WIDE, LANES):
                e = jnp.exp2(s_ref[j, c, p:p + LANES] - m)
                total = total + e
                es.append(e)
            l_ref[c] = total
            o_ref[c] += nt(jnp.concatenate(es, axis=1).astype(BF), vt_ref[j])
        if more:
            decode(j + 1, tv_ref, next_ref)
            vt_ref[j + 1] = next_ref[...]
        return 0

    lax.fori_loop(0, last, lambda j, _: step_b(j, True), 0)
    step_b(last, False)
    dq_ref[...] = jnp.zeros((rows, HD), F32)
    acc_ref[...] = jnp.zeros(acc_ref.shape, F32)
    for ref in (w_refs[-1], d_refs[-1], *x_refs[-2:]):
        ref[...] = jnp.zeros(ref.shape, BF)
    for c in chunks:
        total = jnp.sum(l_ref[c], axis=1, keepdims=True)
        out = (o_ref[c] / total).astype(BF)
        attn_ref[c] = out
        fix = jnp.sum(g_ref[c].astype(F32) * out.astype(F32), axis=1, keepdims=True)
        c_ref[c] = jnp.broadcast_to(fix, (CHUNK, LANES))
        m_ref[c] = m_ref[c] + jnp.log2(total)

    hi_iota = lax.broadcasted_iota(jnp.int32, (64, TILE), 0).astype(F32).astype(BF)
    one, zero = jnp.ones((64, TILE), BF), jnp.zeros((64, TILE), BF)
    zx = jnp.zeros((2 * COLS, TILE), BF)

    def code_sums(j, p):
        base = (j * WIDE + p * TILE) // LANES
        codes = jnp.concatenate([codes_ref[base + i] for i in range(TILE // LANES)], axis=1)
        high = (((codes >> 2) & 1) * 32 + (codes >> 4) * 2 + ((codes >> 3) & 1)).astype(F32).astype(BF)
        low = (codes & 3).astype(F32).astype(BF)
        for grp in range(4):
            his, xs = [], []
            for s in range(4 * grp, 4 * grp + 4):
                his.append(jnp.where(hi_iota == jnp.broadcast_to(high[s:s + 1], (64, TILE)), one, zero))
                x = x_refs[p][s * 16:(s + 1) * 16]
                lo = jnp.broadcast_to(low[s:s + 1], (16, TILE))
                for v in range(4):
                    xs.append(jnp.where(lo == jnp.full((16, TILE), v, BF), x, zx))
            acc_ref[grp] += nt(jnp.concatenate(his, axis=0), jnp.concatenate(xs, axis=0))

    def slopes(j, p):
        for c in chunks:
            lse, fix = m_ref[c], c_ref[c]
            w = jnp.exp2(s_ref[j, c, parts[p]] - jnp.concatenate([lse] * (TILE // LANES), axis=1))
            dp = nn(g_ref[c], vt_ref[j, :, parts[p]])
            w_refs[p][c] = w.astype(BF)
            d_refs[p][c] = (w * (dp - jnp.concatenate([fix] * (TILE // LANES), axis=1))).astype(BF)

    def products(j, p):
        for c in chunks:
            dq_ref[c] += nt(d_refs[p][c], kt_ref[j, :, parts[p]])
        dv = nn(gt_ref[...], w_refs[p][...])
        dk = nn(qt_ref[...], d_refs[p][...]) * SCALE
        for s in range(SUB):
            r = slice(s * COLS, (s + 1) * COLS)
            x_refs[p][s * 16:(s + 1) * 16] = jnp.concatenate([dk[r], dv[r]], axis=0).astype(BF)

    def step_c(j, _):
        before = jnp.maximum(j - 1, 0)
        for p in range(PARTS):
            code_sums(before if p < 2 else j, (p - 2) % PARTS)
            products(before if p < 1 else j, (p - 1) % PARTS)
            slopes(j, p)
        return 0

    lax.fori_loop(0, n_all, step_c, 0)
    products(last, PARTS - 1)
    code_sums(last, PARTS - 2)
    code_sums(last, PARTS - 1)
    qg_ref[...] = (dq_ref[...] * SCALE).astype(BF)
    for s in range(SUB):
        at = s % 4 * 64
        a = acc_ref[s // 4, at:at + 64, at:at + 64].astype(BF)
        book_ref[s * 32:(s + 1) * 32] = jnp.concatenate([a[:32], a[32:]], axis=1)


def attend(q, g, codes, bk, bv):
    rows = q.shape[0]
    tiles = codes.shape[0] * LANES // WIDE
    vm = pl.BlockSpec(memory_space=pltpu.VMEM)
    return pl.pallas_call(
        kernel,
        out_shape=(jax.ShapeDtypeStruct((rows, HD), BF), jax.ShapeDtypeStruct((rows, HD), BF),
                   jax.ShapeDtypeStruct((2 * CODES, HD), BF)),
        in_specs=[vm] * 5,
        out_specs=[vm] * 3,
        scratch_shapes=[
            pltpu.VMEM((tiles, rows, WIDE), F32),
            pltpu.VMEM((tiles, HD, WIDE), BF),
            pltpu.VMEM((tiles, HD, WIDE), BF),
            pltpu.VMEM((HD, WIDE), BF),
            pltpu.VMEM((HD, CODES), F32),
            pltpu.VMEM((HD, CODES), F32),
            pltpu.VMEM((rows, LANES), F32),
            pltpu.VMEM((rows, LANES), F32),
            pltpu.VMEM((rows, LANES), F32),
            pltpu.VMEM((rows, HD), F32),
            pltpu.VMEM((rows, HD), F32),
            pltpu.VMEM((4, 256, 256), F32),
            pltpu.VMEM((HD, rows), BF),
            pltpu.VMEM((HD, rows), BF),
        ]
        + [pltpu.VMEM((rows, TILE), BF)] * (2 * PARTS)
        + [pltpu.VMEM((CODES, TILE), BF)] * PARTS,
        compiler_params=pltpu.CompilerParams(vmem_limit_bytes=48 * 1024 * 1024),
    )(q, g, codes, bk, bv)


def gather_sums(parts_ref, k_ref, v_ref):
    n = parts_ref.shape[0]
    pair = n // KVH
    row = lax.broadcasted_iota(jnp.int32, (KVH, n), 1)
    head = lax.broadcasted_iota(jnp.int32, (KVH, n), 0)
    src = lax.broadcasted_iota(jnp.int32, (HD, 4 * HD), 0)
    dst = lax.broadcasted_iota(jnp.int32, (HD, 4 * HD), 1)
    want = src // 8 % 2 * 256 + dst // 128 % 2 * 128 + src % 8 * 16 + dst // 128 % 2 * 8 + src // 16
    placed = nn(parts_ref[...], (dst == want).astype(F32).astype(BF)).astype(BF)
    for side, out in enumerate((k_ref, v_ref)):
        total = jnp.zeros((KVH, HD), F32)
        for k in range(2):
            pick = ((row // pair == head) & (row % 2 == k)).astype(F32).astype(BF)
            at = (2 * side + k) * HD
            total += nn(pick, placed[:, at:at + HD])
        for j in range(COLS):
            out[:, j, :] = total[:, j * 16:(j + 1) * 16]


def finish(parts):
    vm = pl.BlockSpec(memory_space=pltpu.VMEM)
    shape = jax.ShapeDtypeStruct((KVH, COLS, 16), F32)
    return pl.pallas_call(
        gather_sums,
        out_shape=(shape, shape),
        in_specs=[vm],
        out_specs=(vm, vm),
        compiler_params=pltpu.CompilerParams(vmem_limit_bytes=4 * 1024 * 1024),
    )(parts)


def per_device(queries, codes, codebook_k, codebook_v, grad_out):
    row_count, head_count, columns = queries.shape
    n_ctx, n_head = lax.axis_size("ctx"), lax.axis_size("head")
    kv = lax.axis_index("head") * head_count // GROUP
    own_codes = lax.dynamic_slice_in_dim(codes, kv * SUB, SUB, 1)
    own_codes = own_codes.reshape(row_count // LANES, LANES, SUB).transpose(0, 2, 1)
    own_codes = own_codes.reshape(-1, LANES).astype(BF)
    spread = jnp.broadcast_to(own_codes[None], (n_ctx,) + own_codes.shape)
    all_codes = lax.all_to_all(spread, "ctx", 0, 0, tiled=True).astype(jnp.int32).reshape(-1, SUB, LANES)
    attention, query_grad, books = attend(
        queries.reshape(-1, columns),
        grad_out.reshape(-1, columns),
        all_codes,
        codebook_k,
        codebook_v,
    )
    parts = lax.all_to_all(books.reshape(CODES, 2, columns), ("head", "ctx"), 0, 0, tiled=True)
    sums_k, sums_v = finish(parts.reshape(books.shape))
    return (
        attention.reshape(queries.shape),
        query_grad.reshape(queries.shape),
        sums_k.transpose(0, 2, 1),
        sums_v.transpose(0, 2, 1),
    )


def solution(mesh):
    placed = (P("ctx", "head", None), P("ctx", None), P(), P(), P("ctx", "head", None))
    return jax.shard_map(
        per_device,
        mesh=mesh,
        in_specs=placed,
        out_specs=(
            P("ctx", "head", None),
            P("ctx", "head", None),
            P(None, "ctx", "head"),
            P(None, "ctx", "head"),
        ),
        check_vma=False,
    )
```

```python
import functools
import jax
import jax.numpy as jnp
from jax import lax
from jax.experimental import pallas as pl
from jax.experimental.pallas import tpu as pltpu
from jax.sharding import PartitionSpec as P

KVH = 8
HD = 128
SUB = 16
CODES = 256
GROUP = 4
COLS = HD // SUB
HEADS = 2
TILE = 512
PARTS = 3
WIDE = PARTS * TILE
CHUNK = 384
LANES = 128
NEGATIVE = -1e30
SCALE = HD ** -0.5
LOG2E = 1.4426950408889634
F32 = jnp.float32
BF = jnp.bfloat16


def nn(a, b):
    return lax.dot_general(a, b, (((1,), (0,)), ((), ())), preferred_element_type=F32)


def nt(a, b):
    return lax.dot_general(a, b, (((1,), (1,)), ((), ())), preferred_element_type=F32)


def kernel(q_ref, g_ref, codes_ref, bk_ref, bv_ref, attn_ref, qg_ref, book_ref,
           s_ref, kt_ref, vt_ref, next_ref, tk_ref, tv_ref, m_ref, c_ref, o_ref, dq_ref, acc_ref,
           qt_ref, gt_ref, *bufs):
    rows = q_ref.shape[0]
    own_first = lax.axis_index("ctx") * (rows // HEADS)
    kv = lax.axis_index("head") * HEADS // GROUP
    n_all = (own_first + rows // HEADS + WIDE - 1) // WIDE
    last = n_all - 1
    w_refs, d_refs, x_refs = bufs[:PARTS], bufs[PARTS:2 * PARTS], bufs[2 * PARTS:]
    tk_ref[...] = bk_ref[kv].astype(F32).T
    tv_ref[...] = bv_ref[kv].astype(F32).T
    qt_ref[...] = q_ref[...].astype(F32).T.astype(BF)
    gt_ref[...] = g_ref[...].astype(F32).T.astype(BF)
    m_ref[...] = jnp.full((rows, LANES), NEGATIVE, F32)
    o_ref[...] = jnp.zeros((rows, 2 * HD), F32)
    vt_ref[:, HD:] = jnp.ones((vt_ref.shape[0], HD, WIDE), BF)

    def decode(j, t_ref, out):
        for part in range(WIDE // LANES):
            codes = codes_ref[j * (WIDE // LANES) + part]
            for s in range(SUB):
                idx = jnp.broadcast_to(codes[s:s + 1], (COLS, LANES))
                low = idx & (LANES - 1)
                upper = idx >= LANES
                r = slice(s * COLS, (s + 1) * COLS)
                a = jnp.take_along_axis(t_ref[r, :LANES], low, axis=1, mode="promise_in_bounds")
                b = jnp.take_along_axis(t_ref[r, LANES:], low, axis=1, mode="promise_in_bounds")
                out[r, part * LANES:(part + 1) * LANES] = jnp.where(upper, b, a).astype(BF)

    chunks = [slice(c, c + CHUNK) for c in range(0, rows, CHUNK)]
    parts = [slice(p * TILE, (p + 1) * TILE) for p in range(PARTS)]

    def scores(j, masked):
        for c in chunks:
            top = m_ref[c]
            for p in parts:
                s = nn(q_ref[c], kt_ref[j, :, p]) * (SCALE * LOG2E)
                if masked:
                    u = j * WIDE + p.start + lax.broadcasted_iota(jnp.int32, s.shape, 1)
                    t = own_first + (c.start + lax.broadcasted_iota(jnp.int32, s.shape, 0)) // HEADS
                    s = jnp.where(u <= t, s, NEGATIVE)
                s_ref[j, c, p] = s
                for lane in range(0, TILE, LANES):
                    top = jnp.maximum(top, s[:, lane:lane + LANES])
            m_ref[c] = top

    def step_a(j, _):
        scores(j, False)
        decode(j + 1, tk_ref, next_ref)
        kt_ref[j + 1] = next_ref[...]
        return 0

    decode(0, tk_ref, next_ref)
    kt_ref[0] = next_ref[...]
    lax.fori_loop(0, last, step_a, 0)
    scores(last, True)
    decode(0, tv_ref, next_ref)
    vt_ref[0, :HD] = next_ref[...]
    for c in chunks:
        m_ref[c] = jnp.broadcast_to(jnp.max(m_ref[c], axis=1, keepdims=True), (CHUNK, LANES))

    def step_b(j, more):
        for c in [slice(0, rows)]:
            m = m_ref[c]
            es = []
            for p in range(0, WIDE, LANES):
                e = jnp.exp2(s_ref[j, c, p:p + LANES] - m)
                es.append(e)
            o_ref[c] += nt(jnp.concatenate(es, axis=1).astype(BF), vt_ref[j])
        if more:
            decode(j + 1, tv_ref, next_ref)
            vt_ref[j + 1, :HD] = next_ref[...]
        return 0

    lax.fori_loop(0, last, lambda j, _: step_b(j, True), 0)
    step_b(last, False)
    dq_ref[...] = jnp.zeros((rows, HD), F32)
    acc_ref[...] = jnp.zeros(acc_ref.shape, F32)
    for ref in (w_refs[-1], d_refs[-1], *x_refs[-2:]):
        ref[...] = jnp.zeros(ref.shape, BF)
    for c in chunks:
        total = o_ref[c, HD:]
        out = (o_ref[c, :HD] / total).astype(BF)
        attn_ref[c] = out
        fix = jnp.sum(g_ref[c].astype(F32) * out.astype(F32), axis=1, keepdims=True)
        c_ref[c] = jnp.broadcast_to(fix, (CHUNK, LANES))
        m_ref[c] = m_ref[c] + jnp.log2(total)

    hi_iota = lax.broadcasted_iota(jnp.int32, (64, TILE), 0).astype(F32).astype(BF)
    one, zero = jnp.ones((64, TILE), BF), jnp.zeros((64, TILE), BF)
    zx = jnp.zeros((2 * COLS, TILE), BF)

    def code_sums(j, p):
        base = (j * WIDE + p * TILE) // LANES
        codes = jnp.concatenate([codes_ref[base + i] for i in range(TILE // LANES)], axis=1)
        high = (((codes >> 2) & 1) * 32 + (codes >> 4) * 2 + ((codes >> 3) & 1)).astype(F32).astype(BF)
        low = (codes & 3).astype(F32).astype(BF)
        for grp in range(4):
            his, xs = [], []
            for s in range(4 * grp, 4 * grp + 4):
                his.append(jnp.where(hi_iota == jnp.broadcast_to(high[s:s + 1], (64, TILE)), one, zero))
                x = x_refs[p][s * 16:(s + 1) * 16]
                lo = jnp.broadcast_to(low[s:s + 1], (16, TILE))
                for v in range(4):
                    xs.append(jnp.where(lo == jnp.full((16, TILE), v, BF), x, zx))
            acc_ref[grp] += nt(jnp.concatenate(his, axis=0), jnp.concatenate(xs, axis=0))

    def slopes(j, p):
        for c in chunks:
            lse, fix = m_ref[c], c_ref[c]
            w = jnp.exp2(s_ref[j, c, parts[p]] - jnp.concatenate([lse] * (TILE // LANES), axis=1))
            dp = nn(g_ref[c], vt_ref[j, :HD, parts[p]])
            w_refs[p][c] = w.astype(BF)
            d_refs[p][c] = (w * (dp - jnp.concatenate([fix] * (TILE // LANES), axis=1))).astype(BF)

    def products(j, p):
        for c in chunks:
            dq_ref[c] += nt(d_refs[p][c], kt_ref[j, :, parts[p]])
        dv = nn(gt_ref[...], w_refs[p][...])
        dk = nn(qt_ref[...], d_refs[p][...]) * SCALE
        for s in range(SUB):
            r = slice(s * COLS, (s + 1) * COLS)
            x_refs[p][s * 16:(s + 1) * 16] = jnp.concatenate([dk[r], dv[r]], axis=0).astype(BF)

    def step_c(j, _):
        before = jnp.maximum(j - 1, 0)
        for p in range(PARTS):
            code_sums(before if p < 2 else j, (p - 2) % PARTS)
            products(before if p < 1 else j, (p - 1) % PARTS)
            slopes(j, p)
        return 0

    lax.fori_loop(0, n_all, step_c, 0)
    products(last, PARTS - 1)
    code_sums(last, PARTS - 2)
    code_sums(last, PARTS - 1)
    qg_ref[...] = (dq_ref[...] * SCALE).astype(BF)
    for s in range(SUB):
        at = s % 4 * 64
        a = acc_ref[s // 4, at:at + 64, at:at + 64].astype(BF)
        book_ref[s * 32:(s + 1) * 32] = jnp.concatenate([a[:32], a[32:]], axis=1)


def attend(q, g, codes, bk, bv):
    rows = q.shape[0]
    tiles = codes.shape[0] * LANES // WIDE
    vm = pl.BlockSpec(memory_space=pltpu.VMEM)
    return pl.pallas_call(
        kernel,
        out_shape=(jax.ShapeDtypeStruct((rows, HD), BF), jax.ShapeDtypeStruct((rows, HD), BF),
                   jax.ShapeDtypeStruct((2 * CODES, HD), BF)),
        in_specs=[vm] * 5,
        out_specs=[vm] * 3,
        scratch_shapes=[
            pltpu.VMEM((tiles, rows, WIDE), F32),
            pltpu.VMEM((tiles, HD, WIDE), BF),
            pltpu.VMEM((tiles, 2 * HD, WIDE), BF),
            pltpu.VMEM((HD, WIDE), BF),
            pltpu.VMEM((HD, CODES), F32),
            pltpu.VMEM((HD, CODES), F32),
            pltpu.VMEM((rows, LANES), F32),
            pltpu.VMEM((rows, LANES), F32),
            pltpu.VMEM((rows, 2 * HD), F32),
            pltpu.VMEM((rows, HD), F32),
            pltpu.VMEM((4, 256, 256), F32),
            pltpu.VMEM((HD, rows), BF),
            pltpu.VMEM((HD, rows), BF),
        ]
        + [pltpu.VMEM((rows, TILE), BF)] * (2 * PARTS)
        + [pltpu.VMEM((CODES, TILE), BF)] * PARTS,
        compiler_params=pltpu.CompilerParams(vmem_limit_bytes=48 * 1024 * 1024),
    )(q, g, codes, bk, bv)


def gather_sums(parts_ref, k_ref, v_ref):
    n = parts_ref.shape[0]
    pair = n // KVH
    row = lax.broadcasted_iota(jnp.int32, (KVH, n), 1)
    head = lax.broadcasted_iota(jnp.int32, (KVH, n), 0)
    src = lax.broadcasted_iota(jnp.int32, (HD, 4 * HD), 0)
    dst = lax.broadcasted_iota(jnp.int32, (HD, 4 * HD), 1)
    want = src // 8 % 2 * 256 + dst // 128 % 2 * 128 + src % 8 * 16 + dst // 128 % 2 * 8 + src // 16
    placed = nn(parts_ref[...], (dst == want).astype(F32).astype(BF)).astype(BF)
    for side, out in enumerate((k_ref, v_ref)):
        total = jnp.zeros((KVH, HD), F32)
        for k in range(2):
            pick = ((row // pair == head) & (row % 2 == k)).astype(F32).astype(BF)
            at = (2 * side + k) * HD
            total += nn(pick, placed[:, at:at + HD])
        for j in range(COLS):
            out[:, j, :] = total[:, j * 16:(j + 1) * 16]


def finish(parts):
    vm = pl.BlockSpec(memory_space=pltpu.VMEM)
    shape = jax.ShapeDtypeStruct((KVH, COLS, 16), F32)
    return pl.pallas_call(
        gather_sums,
        out_shape=(shape, shape),
        in_specs=[vm],
        out_specs=(vm, vm),
        compiler_params=pltpu.CompilerParams(vmem_limit_bytes=4 * 1024 * 1024),
    )(parts)


def per_device(queries, codes, codebook_k, codebook_v, grad_out):
    row_count, head_count, columns = queries.shape
    n_ctx, n_head = lax.axis_size("ctx"), lax.axis_size("head")
    kv = lax.axis_index("head") * head_count // GROUP
    own_codes = lax.dynamic_slice_in_dim(codes, kv * SUB, SUB, 1)
    own_codes = own_codes.reshape(row_count // LANES, LANES, SUB).transpose(0, 2, 1)
    own_codes = own_codes.reshape(-1, LANES).astype(BF)
    spread = jnp.broadcast_to(own_codes[None], (n_ctx,) + own_codes.shape)
    all_codes = lax.all_to_all(spread, "ctx", 0, 0, tiled=True).astype(jnp.int32).reshape(-1, SUB, LANES)
    attention, query_grad, books = attend(
        queries.reshape(-1, columns),
        grad_out.reshape(-1, columns),
        all_codes,
        codebook_k,
        codebook_v,
    )
    parts = lax.all_to_all(books.reshape(CODES, 2, columns), ("head", "ctx"), 0, 0, tiled=True)
    sums_k, sums_v = finish(parts.reshape(books.shape))
    return (
        attention.reshape(queries.shape),
        query_grad.reshape(queries.shape),
        sums_k.transpose(0, 2, 1),
        sums_v.transpose(0, 2, 1),
    )


def solution(mesh):
    placed = (P("ctx", "head", None), P("ctx", None), P(), P(), P("ctx", "head", None))
    return jax.shard_map(
        per_device,
        mesh=mesh,
        in_specs=placed,
        out_specs=(
            P("ctx", "head", None),
            P("ctx", "head", None),
            P(None, "ctx", "head"),
            P(None, "ctx", "head"),
        ),
        check_vma=False,
    )
```

```python
import functools
import jax
import jax.numpy as jnp
from jax import lax
from jax.experimental import pallas as pl
from jax.experimental.pallas import tpu as pltpu
from jax.sharding import Mesh, PartitionSpec as P

KVH = 8
HD = 128
SUB = 16
CODES = 256
GROUP = 4
COLS = HD // SUB
HEADS = 2
TILE = 512
PARTS = 3
WIDE = PARTS * TILE
CHUNK = 384
LANES = 128
NEGATIVE = -1e30
SCALE = HD ** -0.5
LOG2E = 1.4426950408889634
F32 = jnp.float32
BF = jnp.bfloat16


def nn(a, b):
    return lax.dot_general(a, b, (((1,), (0,)), ((), ())), preferred_element_type=F32)


def nt(a, b):
    return lax.dot_general(a, b, (((1,), (1,)), ((), ())), preferred_element_type=F32)


def kernel(q_ref, g_ref, codes_ref, bk_ref, bv_ref, attn_ref, qg_ref, book_ref,
           s_ref, kt_ref, vt_ref, next_ref, tk_ref, tv_ref, m_ref, c_ref, o_ref, dq_ref, acc_ref,
           qt_ref, gt_ref, *bufs):
    rows = q_ref.shape[0]
    own_first = lax.axis_index("ctx") * (rows // HEADS)
    kv = lax.axis_index("pair")
    core = lax.axis_index("core")
    n_all = (own_first + rows // HEADS + WIDE - 1) // WIDE
    last = n_all - 1
    w_refs, d_refs, x_refs = bufs[:PARTS], bufs[PARTS:2 * PARTS], bufs[2 * PARTS:]
    tk_ref[...] = bk_ref[kv].astype(F32).T
    tv_ref[...] = bv_ref[kv].astype(F32).T
    qt_ref[...] = q_ref[...].astype(F32).T.astype(BF)
    gt_ref[...] = g_ref[...].astype(F32).T.astype(BF)
    m_ref[...] = jnp.full((rows, LANES), NEGATIVE, F32)
    o_ref[...] = jnp.zeros((rows, 2 * HD), F32)
    vt_ref[:, HD:] = jnp.ones((vt_ref.shape[0], HD, WIDE), BF)

    def decode(j, t_ref, out):
        for part in range(WIDE // LANES):
            codes = codes_ref[j * (WIDE // LANES) + part]
            for s in range(SUB):
                idx = jnp.broadcast_to(codes[s:s + 1], (COLS, LANES))
                low = idx & (LANES - 1)
                upper = idx >= LANES
                r = slice(s * COLS, (s + 1) * COLS)
                a = jnp.take_along_axis(t_ref[r, :LANES], low, axis=1, mode="promise_in_bounds")
                b = jnp.take_along_axis(t_ref[r, LANES:], low, axis=1, mode="promise_in_bounds")
                out[r, part * LANES:(part + 1) * LANES] = jnp.where(upper, b, a).astype(BF)

    chunks = [slice(c, c + CHUNK) for c in range(0, rows, CHUNK)]
    parts = [slice(p * TILE, (p + 1) * TILE) for p in range(PARTS)]

    def scores(j, masked):
        for c in chunks:
            top = m_ref[c]
            for p in parts:
                s = nn(q_ref[c], kt_ref[j, :, p]) * (SCALE * LOG2E)
                if masked:
                    u = j * WIDE + p.start + lax.broadcasted_iota(jnp.int32, s.shape, 1)
                    t = own_first + (c.start + lax.broadcasted_iota(jnp.int32, s.shape, 0)) // HEADS
                    s = jnp.where(u <= t, s, NEGATIVE)
                s_ref[j, c, p] = s
                for lane in range(0, TILE, LANES):
                    top = jnp.maximum(top, s[:, lane:lane + LANES])
            m_ref[c] = top

    def step_a(j, _):
        scores(j, False)
        decode(j + 1, tk_ref, next_ref)
        kt_ref[j + 1] = next_ref[...]
        return 0

    decode(0, tk_ref, next_ref)
    kt_ref[0] = next_ref[...]
    lax.fori_loop(0, last, step_a, 0)
    scores(last, True)
    decode(0, tv_ref, next_ref)
    vt_ref[0, :HD] = next_ref[...]
    for c in chunks:
        m_ref[c] = jnp.broadcast_to(jnp.max(m_ref[c], axis=1, keepdims=True), (CHUNK, LANES))

    def step_b(j, more):
        for c in [slice(0, rows)]:
            m = m_ref[c]
            es = []
            for p in range(0, WIDE, LANES):
                e = jnp.exp2(s_ref[j, c, p:p + LANES] - m)
                es.append(e)
            o_ref[c] += nt(jnp.concatenate(es, axis=1).astype(BF), vt_ref[j])
        if more:
            decode(j + 1, tv_ref, next_ref)
            vt_ref[j + 1, :HD] = next_ref[...]
        return 0

    lax.fori_loop(0, last, lambda j, _: step_b(j, True), 0)
    step_b(last, False)
    dq_ref[...] = jnp.zeros((rows, HD), F32)
    acc_ref[...] = jnp.zeros(acc_ref.shape, F32)
    for ref in (w_refs[-1], d_refs[-1], *x_refs[-2:]):
        ref[...] = jnp.zeros(ref.shape, BF)
    for c in chunks:
        total = o_ref[c, HD:]
        out = (o_ref[c, :HD] / total).astype(BF)
        attn_ref[c] = out
        fix = jnp.sum(g_ref[c].astype(F32) * out.astype(F32), axis=1, keepdims=True)
        c_ref[c] = jnp.broadcast_to(fix, (CHUNK, LANES))
        m_ref[c] = m_ref[c] + jnp.log2(total)

    hi_iota = lax.broadcasted_iota(jnp.int32, (64, TILE), 0).astype(F32).astype(BF)
    one, zero = jnp.ones((64, TILE), BF), jnp.zeros((64, TILE), BF)
    zx = jnp.zeros((2 * COLS, TILE), BF)

    def code_sums(j, p):
        base = (j * WIDE + p * TILE) // LANES
        codes = jnp.concatenate([codes_ref[base + i] for i in range(TILE // LANES)], axis=1)
        high = (((codes >> 2) & 1) * 32 + (codes >> 4) * 2 + ((codes >> 3) & 1)).astype(F32).astype(BF)
        low = (codes & 3).astype(F32).astype(BF)
        for grp in range(4):
            his, xs = [], []
            for s in range(4 * grp, 4 * grp + 4):
                his.append(jnp.where(hi_iota == jnp.broadcast_to(high[s:s + 1], (64, TILE)), one, zero))
                x = x_refs[p][s * 16:(s + 1) * 16]
                lo = jnp.broadcast_to(low[s:s + 1], (16, TILE))
                for v in range(4):
                    xs.append(jnp.where(lo == jnp.full((16, TILE), v, BF), x, zx))
            acc_ref[grp] += nt(jnp.concatenate(his, axis=0), jnp.concatenate(xs, axis=0))

    def slopes(j, p):
        for c in chunks:
            lse, fix = m_ref[c], c_ref[c]
            w = jnp.exp2(s_ref[j, c, parts[p]] - jnp.concatenate([lse] * (TILE // LANES), axis=1))
            dp = nn(g_ref[c], vt_ref[j, :HD, parts[p]])
            w_refs[p][c] = w.astype(BF)
            d_refs[p][c] = (w * (dp - jnp.concatenate([fix] * (TILE // LANES), axis=1))).astype(BF)

    def products(j, p):
        for c in chunks:
            dq_ref[c] += nt(d_refs[p][c], kt_ref[j, :, parts[p]])
        dv = nn(gt_ref[...], w_refs[p][...])
        dk = nn(qt_ref[...], d_refs[p][...]) * SCALE
        for s in range(SUB):
            r = slice(s * COLS, (s + 1) * COLS)
            x_refs[p][s * 16:(s + 1) * 16] = jnp.concatenate([dk[r], dv[r]], axis=0).astype(BF)

    def step_c(j, _):
        before = jnp.maximum(j - 1, 0)
        for p in range(PARTS):
            code_sums(before if p < 2 else j, (p - 2) % PARTS)
            products(before if p < 1 else j, (p - 1) % PARTS)
            slopes(j, p)
        return 0

    lax.fori_loop(0, n_all, step_c, 0)
    products(last, PARTS - 1)
    code_sums(last, PARTS - 2)
    code_sums(last, PARTS - 1)
    qg_ref[...] = (dq_ref[...] * SCALE).astype(BF)
    for s in range(SUB):
        at = s % 4 * 64
        a = acc_ref[s // 4, at:at + 64, at:at + 64].astype(BF)
        to = (s + core) % 2 * CODES + s // 2 * 32
        book_ref[pl.ds(pl.multiple_of(to, 32), 32)] = jnp.concatenate([a[:32], a[32:]], axis=1)


def attend(q, g, codes, bk, bv):
    rows = q.shape[0]
    tiles = codes.shape[0] * LANES // WIDE
    vm = pl.BlockSpec(memory_space=pltpu.VMEM)
    return pl.pallas_call(
        kernel,
        out_shape=(jax.ShapeDtypeStruct((rows, HD), BF), jax.ShapeDtypeStruct((rows, HD), BF),
                   jax.ShapeDtypeStruct((2 * CODES, HD), BF)),
        in_specs=[vm] * 5,
        out_specs=[vm] * 3,
        scratch_shapes=[
            pltpu.VMEM((tiles, rows, WIDE), F32),
            pltpu.VMEM((tiles, HD, WIDE), BF),
            pltpu.VMEM((tiles, 2 * HD, WIDE), BF),
            pltpu.VMEM((HD, WIDE), BF),
            pltpu.VMEM((HD, CODES), F32),
            pltpu.VMEM((HD, CODES), F32),
            pltpu.VMEM((rows, LANES), F32),
            pltpu.VMEM((rows, LANES), F32),
            pltpu.VMEM((rows, 2 * HD), F32),
            pltpu.VMEM((rows, HD), F32),
            pltpu.VMEM((4, 256, 256), F32),
            pltpu.VMEM((HD, rows), BF),
            pltpu.VMEM((HD, rows), BF),
        ]
        + [pltpu.VMEM((rows, TILE), BF)] * (2 * PARTS)
        + [pltpu.VMEM((CODES, TILE), BF)] * PARTS,
        compiler_params=pltpu.CompilerParams(vmem_limit_bytes=48 * 1024 * 1024),
    )(q, g, codes, bk, bv)


def gather_sums(parts_ref, k_ref, v_ref):
    n = parts_ref.shape[0]
    pair = n // KVH
    row = lax.broadcasted_iota(jnp.int32, (KVH, n), 1)
    head = lax.broadcasted_iota(jnp.int32, (KVH, n), 0)
    src = lax.broadcasted_iota(jnp.int32, (HD, 4 * HD), 0)
    dst = lax.broadcasted_iota(jnp.int32, (HD, 4 * HD), 1)
    want = src // 8 % 2 * 256 + dst // 128 % 2 * 128 + src % 8 * 16 + dst // 128 % 2 * 8 + src // 16
    placed = nn(parts_ref[...], (dst == want).astype(F32).astype(BF)).astype(BF)
    for side, out in enumerate((k_ref, v_ref)):
        total = jnp.zeros((KVH, HD), F32)
        for k in range(2):
            pick = ((row // pair == head) & (row % 2 == k)).astype(F32).astype(BF)
            at = (2 * side + k) * HD
            total += nn(pick, placed[:, at:at + HD])
        for j in range(COLS):
            out[:, j, :] = total[:, j * 16:(j + 1) * 16]


def finish(parts):
    vm = pl.BlockSpec(memory_space=pltpu.VMEM)
    shape = jax.ShapeDtypeStruct((KVH, COLS, 16), F32)
    return pl.pallas_call(
        gather_sums,
        out_shape=(shape, shape),
        in_specs=[vm],
        out_specs=(vm, vm),
        compiler_params=pltpu.CompilerParams(vmem_limit_bytes=4 * 1024 * 1024),
    )(parts)


def per_device(queries, codes, codebook_k, codebook_v, grad_out):
    row_count, head_count, columns = queries.shape
    n_ctx = lax.axis_size("ctx")
    kv = lax.axis_index("pair")
    own_codes = lax.dynamic_slice_in_dim(codes, kv * SUB, SUB, 1)
    own_codes = own_codes.reshape(row_count // LANES, LANES, SUB).transpose(0, 2, 1)
    own_codes = own_codes.reshape(-1, LANES).astype(BF)
    spread = jnp.broadcast_to(own_codes[None], (n_ctx,) + own_codes.shape)
    all_codes = lax.all_to_all(spread, "ctx", 0, 0, tiled=True).astype(jnp.int32).reshape(-1, SUB, LANES)
    attention, query_grad, books = attend(
        queries.reshape(-1, columns),
        grad_out.reshape(-1, columns),
        all_codes,
        codebook_k,
        codebook_v,
    )
    own = books[:CODES]
    other = lax.ppermute(books[CODES:], "core", [(0, 1), (1, 0)])
    both = (own.astype(F32) + other.astype(F32)).astype(BF).reshape(CODES // 2, 2, columns)
    parts = lax.all_to_all(both, ("pair", "ctx"), 0, 0, tiled=True)
    sums_k, sums_v = finish(parts.reshape(own.shape))
    return (
        attention.reshape(queries.shape),
        query_grad.reshape(queries.shape),
        sums_k.transpose(0, 2, 1),
        sums_v.transpose(0, 2, 1),
    )


def solution(mesh):
    fine = Mesh(mesh.devices.reshape(mesh.devices.shape[0], -1, 2), ("ctx", "pair", "core"))
    placed = (P("ctx", ("pair", "core"), None), P("ctx", None), P(), P(), P("ctx", ("pair", "core"), None))
    return jax.shard_map(
        per_device,
        mesh=fine,
        in_specs=placed,
        out_specs=(
            P("ctx", ("pair", "core"), None),
            P("ctx", ("pair", "core"), None),
            P(None, "ctx", ("pair", "core")),
            P(None, "ctx", ("pair", "core")),
        ),
        check_vma=False,
    )
```

```python
import functools
import jax
import jax.numpy as jnp
from jax import lax
from jax.experimental import pallas as pl
from jax.experimental.pallas import tpu as pltpu
from jax.sharding import PartitionSpec as P

KVH = 8
HD = 128
SUB = 16
CODES = 256
GROUP = 4
COLS = HD // SUB
HEADS = 2
TILE = 512
PARTS = 3
WIDE = PARTS * TILE
CHUNK = 384
LANES = 128
NEGATIVE = -1e30
SCALE = HD ** -0.5
LOG2E = 1.4426950408889634
F32 = jnp.float32
BF = jnp.bfloat16


def nn(a, b):
    return lax.dot_general(a, b, (((1,), (0,)), ((), ())), preferred_element_type=F32)


def nt(a, b):
    return lax.dot_general(a, b, (((1,), (1,)), ((), ())), preferred_element_type=F32)


def kernel(q_ref, g_ref, codes_ref, bk_ref, bv_ref, attn_ref, qg_ref, book_ref,
           s_ref, kt_ref, vt_ref, next_ref, tk_ref, tv_ref, m_ref, c_ref, o_ref, dq_ref, acc_ref,
           qt_ref, gt_ref, *bufs):
    rows = q_ref.shape[0]
    own_first = lax.axis_index("ctx") * (rows // HEADS)
    kv = lax.axis_index("head") * HEADS // GROUP
    n_all = (own_first + rows // HEADS + WIDE - 1) // WIDE
    last = n_all - 1
    w_refs, d_refs, x_refs = bufs[:PARTS], bufs[PARTS:2 * PARTS], bufs[2 * PARTS:]
    tk_ref[...] = bk_ref[kv].astype(F32).T
    tv_ref[...] = bv_ref[kv].astype(F32).T
    qt_ref[...] = q_ref[...].astype(F32).T.astype(BF)
    gt_ref[...] = g_ref[...].astype(F32).T.astype(BF)
    m_ref[...] = jnp.full((rows, LANES), NEGATIVE, F32)
    o_ref[...] = jnp.zeros((rows, 2 * HD), F32)
    vt_ref[:, HD:] = jnp.ones((vt_ref.shape[0], HD, WIDE), BF)

    def decode(j, t_ref, out):
        for part in range(WIDE // LANES):
            codes = codes_ref[j * (WIDE // LANES) + part]
            for s in range(SUB):
                idx = jnp.broadcast_to(codes[s:s + 1], (COLS, LANES))
                low = idx & (LANES - 1)
                upper = idx >= LANES
                r = slice(s * COLS, (s + 1) * COLS)
                a = jnp.take_along_axis(t_ref[r, :LANES], low, axis=1, mode="promise_in_bounds")
                b = jnp.take_along_axis(t_ref[r, LANES:], low, axis=1, mode="promise_in_bounds")
                out[r, part * LANES:(part + 1) * LANES] = jnp.where(upper, b, a).astype(BF)

    whole = [slice(0, rows)]
    chunks = [slice(c, c + CHUNK) for c in range(0, rows, CHUNK)]
    parts = [slice(p * TILE, (p + 1) * TILE) for p in range(PARTS)]

    def scores(j, masked):
        for c in whole:
            top = m_ref[c]
            for p in parts:
                s = nn(q_ref[c], kt_ref[j, :, p]) * (SCALE * LOG2E)
                if masked:
                    u = j * WIDE + p.start + lax.broadcasted_iota(jnp.int32, s.shape, 1)
                    t = own_first + (c.start + lax.broadcasted_iota(jnp.int32, s.shape, 0)) // HEADS
                    s = jnp.where(u <= t, s, NEGATIVE)
                s_ref[j, c, p] = s
                for lane in range(0, TILE, LANES):
                    top = jnp.maximum(top, s[:, lane:lane + LANES])
            m_ref[c] = top

    def step_a(j, _):
        scores(j, False)
        decode(j + 1, tk_ref, next_ref)
        kt_ref[j + 1] = next_ref[...]
        return 0

    decode(0, tk_ref, next_ref)
    kt_ref[0] = next_ref[...]
    lax.fori_loop(0, last, step_a, 0)
    scores(last, True)
    decode(0, tv_ref, next_ref)
    vt_ref[0, :HD] = next_ref[...]
    for c in chunks:
        m_ref[c] = jnp.broadcast_to(jnp.max(m_ref[c], axis=1, keepdims=True), (CHUNK, LANES))

    def step_b(j, more):
        for c in whole:
            m = m_ref[c]
            es = []
            for p in range(0, WIDE, LANES):
                e = jnp.exp2(s_ref[j, c, p:p + LANES] - m)
                es.append(e)
            o_ref[c] += nt(jnp.concatenate(es, axis=1).astype(BF), vt_ref[j])
        if more:
            decode(j + 1, tv_ref, next_ref)
            vt_ref[j + 1, :HD] = next_ref[...]
        return 0

    lax.fori_loop(0, last, lambda j, _: step_b(j, True), 0)
    step_b(last, False)
    dq_ref[...] = jnp.zeros((rows, HD), F32)
    acc_ref[...] = jnp.zeros(acc_ref.shape, F32)
    for ref in (w_refs[-1], d_refs[-1], *x_refs[-2:]):
        ref[...] = jnp.zeros(ref.shape, BF)
    for c in chunks:
        total = o_ref[c, HD:]
        out = (o_ref[c, :HD] / total).astype(BF)
        attn_ref[c] = out
        fix = jnp.sum(g_ref[c].astype(F32) * out.astype(F32), axis=1, keepdims=True)
        fix = jnp.broadcast_to(-fix, (CHUNK, LANES))
        lane = lax.broadcasted_iota(jnp.int32, fix.shape, 1)
        first = fix.astype(BF).astype(F32)
        second = (fix - first).astype(BF).astype(F32)
        third = fix - first - second
        terms = jnp.where(lane == 0, first, jnp.where(lane == 1, second, jnp.where(lane == 2, third, 0.0)))
        c_ref[c] = jnp.concatenate([g_ref[c], terms.astype(BF)], axis=1)
        m_ref[c] = m_ref[c] + jnp.log2(total)

    hi_iota = lax.broadcasted_iota(jnp.int32, (64, TILE), 0).astype(F32).astype(BF)
    one, zero = jnp.ones((64, TILE), BF), jnp.zeros((64, TILE), BF)
    zx = jnp.zeros((2 * COLS, TILE), BF)

    def code_sums(j, p):
        base = (j * WIDE + p * TILE) // LANES
        codes = jnp.concatenate([codes_ref[base + i] for i in range(TILE // LANES)], axis=1)
        high = (((codes >> 2) & 1) * 32 + (codes >> 4) * 2 + ((codes >> 3) & 1)).astype(F32).astype(BF)
        low = (codes & 3).astype(F32).astype(BF)
        for grp in range(4):
            his, xs = [], []
            for s in range(4 * grp, 4 * grp + 4):
                his.append(jnp.where(hi_iota == jnp.broadcast_to(high[s:s + 1], (64, TILE)), one, zero))
                x = x_refs[p][s * 16:(s + 1) * 16]
                lo = jnp.broadcast_to(low[s:s + 1], (16, TILE))
                for v in range(4):
                    xs.append(jnp.where(lo == jnp.full((16, TILE), v, BF), x, zx))
            acc_ref[grp] += nt(jnp.concatenate(his, axis=0), jnp.concatenate(xs, axis=0))

    def slopes(j, p):
        for c in whole:
            lse = m_ref[c]
            w = jnp.exp2(s_ref[j, c, parts[p]] - jnp.concatenate([lse] * (TILE // LANES), axis=1))
            dp = nn(c_ref[c], vt_ref[j, :, parts[p]])
            w_refs[p][c] = w.astype(BF)
            d_refs[p][c] = (w * dp).astype(BF)

    def products(j, p):
        for c in chunks:
            dq_ref[c] += nt(d_refs[p][c], kt_ref[j, :, parts[p]])
        dv = nn(gt_ref[...], w_refs[p][...])
        dk = nn(qt_ref[...], d_refs[p][...]) * SCALE
        for s in range(SUB):
            r = slice(s * COLS, (s + 1) * COLS)
            x_refs[p][s * 16:(s + 1) * 16] = jnp.concatenate([dk[r], dv[r]], axis=0).astype(BF)

    def step_c(j, _):
        before = jnp.maximum(j - 1, 0)
        for p in range(PARTS):
            code_sums(before if p < 2 else j, (p - 2) % PARTS)
            products(before if p < 1 else j, (p - 1) % PARTS)
            slopes(j, p)
        return 0

    lax.fori_loop(0, n_all, step_c, 0)
    products(last, PARTS - 1)
    code_sums(last, PARTS - 2)
    code_sums(last, PARTS - 1)
    qg_ref[...] = (dq_ref[...] * SCALE).astype(BF)
    for s in range(SUB):
        at = s % 4 * 64
        a = acc_ref[s // 4, at:at + 64, at:at + 64].astype(BF)
        book_ref[s * 32:(s + 1) * 32] = jnp.concatenate([a[:32], a[32:]], axis=1)


def attend(q, g, codes, bk, bv):
    rows = q.shape[0]
    tiles = codes.shape[0] * LANES // WIDE
    vm = pl.BlockSpec(memory_space=pltpu.VMEM)
    return pl.pallas_call(
        kernel,
        out_shape=(jax.ShapeDtypeStruct((rows, HD), BF), jax.ShapeDtypeStruct((rows, HD), BF),
                   jax.ShapeDtypeStruct((2 * CODES, HD), BF)),
        in_specs=[vm] * 5,
        out_specs=[vm] * 3,
        scratch_shapes=[
            pltpu.VMEM((tiles, rows, WIDE), F32),
            pltpu.VMEM((tiles, HD, WIDE), BF),
            pltpu.VMEM((tiles, 2 * HD, WIDE), BF),
            pltpu.VMEM((HD, WIDE), BF),
            pltpu.VMEM((HD, CODES), F32),
            pltpu.VMEM((HD, CODES), F32),
            pltpu.VMEM((rows, LANES), F32),
            pltpu.VMEM((rows, 2 * HD), BF),
            pltpu.VMEM((rows, 2 * HD), F32),
            pltpu.VMEM((rows, HD), F32),
            pltpu.VMEM((4, 256, 256), F32),
            pltpu.VMEM((HD, rows), BF),
            pltpu.VMEM((HD, rows), BF),
        ]
        + [pltpu.VMEM((rows, TILE), BF)] * (2 * PARTS)
        + [pltpu.VMEM((CODES, TILE), BF)] * PARTS,
        compiler_params=pltpu.CompilerParams(vmem_limit_bytes=48 * 1024 * 1024),
    )(q, g, codes, bk, bv)


def gather_sums(parts_ref, k_ref, v_ref):
    n = parts_ref.shape[0]
    pair = n // KVH
    row = lax.broadcasted_iota(jnp.int32, (KVH, n), 1)
    head = lax.broadcasted_iota(jnp.int32, (KVH, n), 0)
    src = lax.broadcasted_iota(jnp.int32, (HD, 4 * HD), 0)
    dst = lax.broadcasted_iota(jnp.int32, (HD, 4 * HD), 1)
    want = src // 8 % 2 * 256 + dst // 128 % 2 * 128 + src % 8 * 16 + dst // 128 % 2 * 8 + src // 16
    placed = nn(parts_ref[...], (dst == want).astype(F32).astype(BF)).astype(BF)
    for side, out in enumerate((k_ref, v_ref)):
        total = jnp.zeros((KVH, HD), F32)
        for k in range(2):
            pick = ((row // pair == head) & (row % 2 == k)).astype(F32).astype(BF)
            at = (2 * side + k) * HD
            total += nn(pick, placed[:, at:at + HD])
        for j in range(COLS):
            out[:, j, :] = total[:, j * 16:(j + 1) * 16]


def finish(parts):
    vm = pl.BlockSpec(memory_space=pltpu.VMEM)
    shape = jax.ShapeDtypeStruct((KVH, COLS, 16), F32)
    return pl.pallas_call(
        gather_sums,
        out_shape=(shape, shape),
        in_specs=[vm],
        out_specs=(vm, vm),
        compiler_params=pltpu.CompilerParams(vmem_limit_bytes=4 * 1024 * 1024),
    )(parts)


def per_device(queries, codes, codebook_k, codebook_v, grad_out):
    row_count, head_count, columns = queries.shape
    n_ctx, n_head = lax.axis_size("ctx"), lax.axis_size("head")
    kv = lax.axis_index("head") * head_count // GROUP
    own_codes = lax.dynamic_slice_in_dim(codes, kv * SUB, SUB, 1)
    own_codes = own_codes.reshape(row_count // LANES, LANES, SUB).transpose(0, 2, 1)
    own_codes = own_codes.reshape(-1, LANES).astype(BF)
    spread = jnp.broadcast_to(own_codes[None], (n_ctx,) + own_codes.shape)
    all_codes = lax.all_to_all(spread, "ctx", 0, 0, tiled=True).astype(jnp.int32).reshape(-1, SUB, LANES)
    attention, query_grad, books = attend(
        queries.reshape(-1, columns),
        grad_out.reshape(-1, columns),
        all_codes,
        codebook_k,
        codebook_v,
    )
    parts = lax.all_to_all(books.reshape(CODES, 2, columns), ("head", "ctx"), 0, 0, tiled=True)
    sums_k, sums_v = finish(parts.reshape(books.shape))
    return (
        attention.reshape(queries.shape),
        query_grad.reshape(queries.shape),
        sums_k.transpose(0, 2, 1),
        sums_v.transpose(0, 2, 1),
    )


def solution(mesh):
    placed = (P("ctx", "head", None), P("ctx", None), P(), P(), P("ctx", "head", None))
    return jax.shard_map(
        per_device,
        mesh=mesh,
        in_specs=placed,
        out_specs=(
            P("ctx", "head", None),
            P("ctx", "head", None),
            P(None, "ctx", "head"),
            P(None, "ctx", "head"),
        ),
        check_vma=False,
    )
```
